32 devices in a mesh: geom: 2 (over x), edge: 4 (over y, core), mode: 4 (over z).
Axes of the slice: x: 2, y: 2, z: 4, core: 2. Of those that a mesh axis runs over, the one named last changes fastest.
Arguments:
- basis: bfloat16 [12288, 1024], P(('geom', 'edge'), 'mode'), parts along dimension 0, may hold values from -6 to 6
- motional: bfloat16 [4, 48, 16, 128, 128], P('geom', 'edge'), parts along dimension 0, may hold values from -0.0017089844 to 0.0017089844
- block_cols: int32 [96, 16], P(('geom', 'edge')), parts along dimension 0, may hold values from 0 to 47, as said below
- block_counts: int32 [96], P(('geom', 'edge')), parts along dimension 0, may hold values from 8 to 16, as said below
Outputs:
- reduced: float32 [4, 1024, 1024], P('geom', 'edge', 'mode'), parts along dimension 0
The draws below stay inside these ranges and needn't reach their ends.
There are 2 independent parts, one for each index of `geom`. The reference program is written for one: setup_inputs(seed, part) draws one part's arguments, and reference() takes and returns one part's arrays. A program takes and returns all parts, laid end to end along the dimension named above; each array names one. Nothing has to cross between parts.
Inputs may be any that keep to these rules, and one draw needn't show every extreme that they name: `block_cols`: block row r's live slots hold distinct block columns within 12 blocks of r (at most r + 12, at least r - 12); slot 0 is r itself; slots at or past block_counts[r] hold r. block_counts[r] never exceeds the number of block columns within 12 blocks of r.
All inputs are finite; a program needn't handle non-finite values.
Results may differ from the reference program's by a relative error of at most 0.0029.
Values may be sent and summed in bfloat16 or wider, within the bound.
A program may use at most 64 MiB of HBM per device.

```python
import jax
import jax.numpy as jnp
from jax import lax

M = 1024
BS = 128
NNZ = 16
NBR_DEV = 12
NBLK = 48
ROWS = 6144


def pattern(key):
    span = 2 * NBR_DEV + 1
    sub = jax.random.fold_in(key, 11)
    raw = jax.random.randint(sub, (NBLK, span), 0, 1 << 20)
    order = jnp.arange(span, dtype=jnp.int32)
    scores = raw * 256 + order[None, :]
    row_index = jnp.arange(NBLK, dtype=jnp.int32)[:, None]
    columns = row_index + order[None, :] - NBR_DEV
    valid = (columns >= 0) & (columns < NBLK)
    scores = jnp.where(order[None, :] == NBR_DEV, 1 << 29, scores)
    scores = jnp.where(valid, scores, -1 - order[None, :])
    top_scores, picks = lax.top_k(scores, NNZ)
    cols = row_index + picks.astype(jnp.int32) - NBR_DEV
    reach = jnp.minimum(NNZ, jnp.sum(valid.astype(jnp.int32), axis=1)).astype(jnp.int32)
    wanted = jax.random.randint(jax.random.fold_in(key, 23), (NBLK,), NNZ // 2, NNZ + 1).astype(jnp.int32)
    rows_flat = jnp.arange(NBLK, dtype=jnp.int32)
    wanted = jnp.where(rows_flat % NBR_DEV == 0, NNZ, wanted)
    count = jnp.minimum(reach, wanted).astype(jnp.int32)
    live = jnp.arange(NNZ, dtype=jnp.int32)[None, :] < count[:, None]
    cols = jnp.where(live, cols, row_index)
    return (cols.astype(jnp.int32), count)


def draw_block_cols(key, part):
    return pattern(key)[0]


def draw_block_counts(key, part):
    return pattern(key)[1]


def steps_of(own_key, extent, cuts, smallest, largest):
    def one(dim, blocks):
        heights = jax.random.uniform(jax.random.fold_in(jax.random.fold_in(own_key, 6), dim), (blocks,), jnp.float32, smallest / len(cuts), largest / len(cuts))
        return jnp.repeat(jnp.exp(heights), extent[dim] // blocks).reshape((-1,) + (1,) * (len(extent) - dim - 1))

    factor_of = one(*cuts[0])
    for cut in cuts[1:]:
        factor_of = factor_of * one(*cut)
    return factor_of


def normal_values(stream_key, extent, width, most, split=(), kind=jnp.bfloat16):
    values = jax.random.normal(stream_key, extent, jnp.float32) * width
    if len(split) > 0:
        values = steps_of(stream_key, extent, split, -0.22, 0.18) * values
    return jnp.clip(values, min=-most, max=most).astype(kind)


def setup_inputs(seed: int = 0, part: int = 0) -> dict:
    keys = jax.random.split(jax.random.key(seed), 5)
    own_keys = jax.random.split(jax.random.fold_in(keys[4], part), 5)
    basis = normal_values(own_keys[0], (ROWS, M), 1.0, 6.0, ((0, 4), (1, 4)))
    motional = normal_values(own_keys[1], (2, NBLK, NNZ, BS, BS), (NNZ * BS * ROWS) ** -0.5, 0.0017089844, ((1, 4),))
    block_cols = draw_block_cols(jax.random.fold_in(jax.random.fold_in(keys[4], part), 71), part)
    block_counts = draw_block_counts(jax.random.fold_in(jax.random.fold_in(keys[4], part), 71), part)
    return {"basis": basis, "motional": motional, "block_cols": block_cols, "block_counts": block_counts}


def reference(basis, motional, block_cols, block_counts):
    nblk = block_cols.shape[0]
    tiles = basis.reshape(nblk, BS, M)
    slots = jnp.arange(NNZ, dtype=jnp.int32)

    def one_row(index):
        cols = block_cols[index]
        live = (slots < block_counts[index]).astype(jnp.float32)
        picked = tiles[cols].astype(jnp.float32) * live[:, None, None]
        blocks = motional[:, index].astype(jnp.float32)
        return jnp.einsum('qkij,kjm->qim', blocks, picked).astype(jnp.bfloat16)

    work = lax.map(one_row, jnp.arange(nblk, dtype=jnp.int32))
    work = jnp.transpose(work, (1, 0, 2, 3)).reshape(2, nblk * BS, M)
    first = jnp.dot(basis.T, work[0], preferred_element_type=jnp.float32)
    second = jnp.dot(basis.T, work[1], preferred_element_type=jnp.float32)
    return jnp.stack([first, second], axis=0)
```

```python
import functools

import jax
import jax.numpy as jnp
from jax import lax
from jax.experimental import pallas as pl
from jax.experimental.pallas import tpu as pltpu
from jax.sharding import PartitionSpec as P

MESH = pl.DeviceIdType.MESH


def kernel(
    n_edge, n_mode,
    cols_ref, counts_ref, basis, motional, out,
    ext, gath, mot, work, mine, to_mate, from_mate, to_chip, from_chip,
    own_sem, mot_sem, halo_send, halo_recv, right_send, right_recv, left_send, left_recv,
    mate_send, mate_recv, chip_send, chip_recv,
):
    edge, mode = lax.axis_index("edge"), lax.axis_index("mode")
    nbr, bs, cl = basis.shape
    nnz = mot.shape[2]
    rows = nbr * bs
    n_chip = n_edge // 2
    share = mine.shape[1]
    per_block = cl // share
    chip, core = lax.div(edge, 2), lax.rem(edge, 2)
    mate = edge + 1 - 2 * core

    barrier = pltpu.get_barrier_semaphore()
    for step in range(1, n_edge):
        pl.semaphore_signal(barrier, inc=1, device_id={"edge": lax.rem(edge + step, n_edge)}, device_id_type=MESH)
    has_left, has_right = mode > 0, mode < n_mode - 1
    has_before, has_after = edge > 0, edge < n_edge - 1

    @pl.when(has_left)
    def _():
        pl.semaphore_signal(barrier, inc=1, device_id={"mode": mode - 1}, device_id_type=MESH)

    @pl.when(has_right)
    def _():
        pl.semaphore_signal(barrier, inc=1, device_id={"mode": mode + 1}, device_id_type=MESH)

    own = [
        pltpu.make_async_copy(basis, ext.at[pl.ds(nbr, nbr)], own_sem.at[0]),
        pltpu.make_async_copy(basis, gath.at[mode], own_sem.at[1]),
    ]

    def mot_copy(r):
        return pltpu.make_async_copy(motional.at[:, r], mot.at[:, r], mot_sem.at[r])

    for copy in own:
        copy.start()
    for r in range(nbr):
        mot_copy(r).start()
    ext[3 * nbr] = jnp.zeros((bs, cl), jnp.bfloat16)

    pl.semaphore_wait(barrier, n_edge - 1 + has_left.astype(jnp.int32) + has_right.astype(jnp.int32))

    def go_right(d):
        block = mode - d
        return pltpu.make_async_remote_copy(
            src_ref=basis if d == 0 else gath.at[block], dst_ref=gath.at[block],
            send_sem=right_send.at[d], recv_sem=right_recv.at[d],
            device_id={"mode": mode + 1}, device_id_type=MESH,
        )

    def go_left(d):
        block = mode + d
        return pltpu.make_async_remote_copy(
            src_ref=basis if d == 0 else gath.at[block], dst_ref=gath.at[block],
            send_sem=left_send.at[d], recv_sem=left_recv.at[d],
            device_id={"mode": mode - 1}, device_id_type=MESH,
        )

    def halo(side):
        return pltpu.make_async_remote_copy(
            src_ref=basis, dst_ref=ext.at[pl.ds(2 * nbr * side, nbr)],
            send_sem=halo_send.at[side], recv_sem=halo_recv.at[side],
            device_id={"edge": edge + 1 - 2 * side}, device_id_type=MESH,
        )

    def landed(dst, sem):
        pltpu.make_async_copy(dst, dst, sem).wait()

    @pl.when(has_after)
    def _():
        halo(0).start()

    @pl.when(has_before)
    def _():
        halo(1).start()

    @pl.when(has_right)
    def _():
        go_right(0).start()

    @pl.when(has_left)
    def _():
        go_left(0).start()

    for copy in own:
        copy.wait()

    @pl.when(has_before)
    def _():
        landed(ext.at[pl.ds(0, nbr)], halo_recv.at[0])

    @pl.when(has_after)
    def _():
        landed(ext.at[pl.ds(2 * nbr, nbr)], halo_recv.at[1])

    first = edge * nbr - nbr

    def block_row(r, carry):
        mot_copy(r).wait()
        count = counts_ref[r]
        tiles = [
            ext[jnp.where(k < count, cols_ref[r, k] - first, 3 * nbr)] for k in range(nnz)
        ]
        rhs = jnp.concatenate(tiles, axis=0)
        at = pl.ds(pl.multiple_of(r * bs, bs), bs)
        for q in range(2):
            lhs = jnp.concatenate([mot[q, r, k] for k in range(nnz)], axis=1)
            product = jnp.dot(lhs, rhs, preferred_element_type=jnp.float32)
            work[at, q * cl:(q + 1) * cl] = product.astype(jnp.bfloat16)
        return carry

    lax.fori_loop(0, nbr, block_row, 0)

    def mate_copy(h):
        return pltpu.make_async_remote_copy(
            src_ref=to_mate.at[h], dst_ref=from_mate.at[h],
            send_sem=mate_send.at[h], recv_sem=mate_recv.at[h],
            device_id={"edge": mate}, device_id_type=MESH,
        )

    def chip_copy(h):
        return pltpu.make_async_remote_copy(
            src_ref=to_chip.at[h], dst_ref=from_chip.at[chip],
            send_sem=chip_send.at[h], recv_sem=chip_recv.at[chip],
            device_id={"edge": 2 * h + core}, device_id_type=MESH,
        )

    def product_of(block):
        left = gath[block].reshape(rows, cl)
        total = lax.dot_general(
            left, work[...], (((0,), (0,)), ((), ())), preferred_element_type=jnp.float32
        )
        for k in range(per_block):
            s = block * per_block + k
            h = lax.div(s, 2)
            part = total[k * share:(k + 1) * share]

            @pl.when(lax.rem(s, 2) != core)
            def _():
                to_mate[h] = part
                mate_copy(h).start()

            @pl.when(lax.rem(s, 2) == core)
            def _():
                mine[h] = part

        for k in range(per_block):
            s = block * per_block + k
            h = lax.div(s, 2)

            @pl.when(lax.rem(s, 2) == core)
            def _():
                landed(from_mate.at[h], mate_recv.at[h])

                @pl.when(h != chip)
                def _():
                    to_chip[h] = mine[h] + from_mate[h]
                    chip_copy(h).start()

    product_of(mode)
    for d in range(1, n_mode):
        @pl.when(mode >= d)
        def _():
            landed(gath.at[mode - d], right_recv.at[d - 1])

            if d < n_mode - 1:
                @pl.when(has_right)
                def _():
                    go_right(d).start()

        @pl.when(mode + d < n_mode)
        def _():
            landed(gath.at[mode + d], left_recv.at[d - 1])

            if d < n_mode - 1:
                @pl.when(has_left)
                def _():
                    go_left(d).start()

        @pl.when(mode >= d)
        def _():
            product_of(mode - d)

        @pl.when(mode + d < n_mode)
        def _():
            product_of(mode + d)

    total = mine[chip] + from_mate[chip]
    for step in range(1, n_chip):
        other = lax.rem(chip + step, n_chip)
        landed(from_chip.at[other], chip_recv.at[other])
        total = total + from_chip[other]
    for q in range(2):
        out[q] = total[:, q * cl:(q + 1) * cl]

    for side, there in ((0, has_after), (1, has_before)):
        @pl.when(there)
        def _():
            halo(side).wait_send()

    for d in range(n_mode - 1):
        @pl.when(has_right & (mode >= d))
        def _():
            go_right(d).wait_send()

        @pl.when(has_left & (mode + d < n_mode))
        def _():
            go_left(d).wait_send()

    for h in range(n_chip):
        mate_copy(h).wait_send()

        @pl.when(h != chip)
        def _():
            chip_copy(h).wait_send()


def per_device(n_edge, n_mode, basis, motional, block_cols, block_counts):
    rows, cl = basis.shape
    nbr, nnz = block_cols.shape
    bs = motional.shape[-1]
    share = cl * n_mode // n_edge
    n_chip = n_edge // 2
    part = (n_chip, share, 2 * cl)
    dma = pltpu.SemaphoreType.DMA
    return pl.pallas_call(
        functools.partial(kernel, n_edge, n_mode),
        out_shape=jax.ShapeDtypeStruct((2, share, cl), jnp.float32),
        in_specs=[
            pl.BlockSpec(memory_space=pltpu.SMEM),
            pl.BlockSpec(memory_space=pltpu.SMEM),
            pl.BlockSpec(memory_space=pl.ANY),
            pl.BlockSpec(memory_space=pl.ANY),
        ],
        out_specs=pl.BlockSpec(memory_space=pltpu.VMEM),
        scratch_shapes=[
            pltpu.VMEM((3 * nbr + 1, bs, cl), jnp.bfloat16),
            pltpu.VMEM((n_mode, nbr, bs, cl), jnp.bfloat16),
            pltpu.VMEM((2, nbr, nnz, bs, bs), jnp.bfloat16),
            pltpu.VMEM((rows, 2 * cl), jnp.bfloat16),
            pltpu.VMEM(part, jnp.float32),
            pltpu.VMEM(part, jnp.float32),
            pltpu.VMEM(part, jnp.float32),
            pltpu.VMEM(part, jnp.float32),
            pltpu.VMEM(part, jnp.float32),
            dma((2,)),
            dma((nbr,)),
            dma((2,)),
            dma((2,)),
            dma((n_mode,)),
            dma((n_mode,)),
            dma((n_mode,)),
            dma((n_mode,)),
            dma((n_chip,)),
            dma((n_chip,)),
            dma((n_chip,)),
            dma((n_chip,)),
        ],
        compiler_params=pltpu.CompilerParams(
            collective_id=0, has_side_effects=True, vmem_limit_bytes=48 * 2**20
        ),
    )(block_cols, block_counts, basis.reshape(nbr, bs, cl), motional)


def solution(mesh):
    placed = (
        P(("geom", "edge"), "mode"),
        P("geom", "edge", None, None, None),
        P(("geom", "edge"), None),
        P(("geom", "edge")),
    )
    return jax.shard_map(
        functools.partial(per_device, mesh.shape["edge"], mesh.shape["mode"]),
        mesh=mesh, in_specs=placed, out_specs=P("geom", "edge", "mode"), check_vma=False,
    )
```

```python
import functools

import jax
import jax.numpy as jnp
from jax import lax
from jax.experimental import pallas as pl
from jax.experimental.pallas import tpu as pltpu
from jax.sharding import PartitionSpec as P

MESH = pl.DeviceIdType.MESH


def kernel(
    n_edge, n_mode,
    cols_ref, counts_ref, basis, motional, out,
    ext_own, ext_end, gath, mot, work, mine, to_mate, from_mate, to_chip, from_chip,
    mine_far, to_mate_far, from_mate_far, to_end, from_helper,
    own_sem, mot_sem, halo_send, halo_recv, right_send, right_recv, left_send, left_recv,
    mate_send, mate_recv, chip_send, chip_recv, far_send, far_recv, end_recv,
):
    ext = (ext_own, ext_end)
    edge, mode = lax.axis_index("edge"), lax.axis_index("mode")
    nbr, bs, cl = basis.shape
    nnz = mot.shape[2]
    rows = nbr * bs
    n_chip = n_edge // 2
    share = mine.shape[1]
    per_block = cl // share
    chip, core = lax.div(edge, 2), lax.rem(edge, 2)
    mate = edge + 1 - 2 * core
    is_end = (mode == 0) | (mode == n_mode - 1)
    is_helper = (mode == 1) | (mode == n_mode - 2)
    low = (mode < 2).astype(jnp.int32)
    end = (n_mode - 1) * (1 - low)
    far = (n_mode - 1) * low
    helper = end + 2 * low - 1

    barrier = pltpu.get_barrier_semaphore()
    for step in range(1, n_edge):
        pl.semaphore_signal(barrier, inc=1, device_id={"edge": lax.rem(edge + step, n_edge)}, device_id_type=MESH)
    has_left, has_right = mode > 0, mode < n_mode - 1
    has_before, has_after = edge > 0, edge < n_edge - 1

    @pl.when(has_left)
    def _():
        pl.semaphore_signal(barrier, inc=1, device_id={"mode": mode - 1}, device_id_type=MESH)

    @pl.when(has_right)
    def _():
        pl.semaphore_signal(barrier, inc=1, device_id={"mode": mode + 1}, device_id_type=MESH)

    for step in range(1, n_edge):
        to = lax.rem(edge + step, n_edge)

        @pl.when(is_end)
        def _():
            pl.semaphore_signal(barrier, inc=1, device_id={"edge": to, "mode": helper}, device_id_type=MESH)

        @pl.when(is_helper)
        def _():
            pl.semaphore_signal(barrier, inc=1, device_id={"edge": to, "mode": end}, device_id_type=MESH)

    own = [
        pltpu.make_async_copy(basis, ext[0].at[pl.ds(nbr, nbr)], own_sem.at[0]),
        pltpu.make_async_copy(basis, gath.at[mode], own_sem.at[1]),
    ]

    def mot_copy(r):
        return pltpu.make_async_copy(motional.at[:, r], mot.at[:, r], mot_sem.at[r])

    for copy in own:
        copy.start()
    for r in range(nbr):
        mot_copy(r).start()
    for g in range(2):
        ext[g][3 * nbr] = jnp.zeros((bs, cl), jnp.bfloat16)

    crossing = (n_edge - 1) * (is_end | is_helper).astype(jnp.int32)
    pl.semaphore_wait(barrier, n_edge - 1 + has_left.astype(jnp.int32) + has_right.astype(jnp.int32) + crossing)

    def go_right(d):
        block = mode - d
        return pltpu.make_async_remote_copy(
            src_ref=basis if d == 0 else gath.at[block], dst_ref=gath.at[block],
            send_sem=right_send.at[d], recv_sem=right_recv.at[d],
            device_id={"mode": mode + 1}, device_id_type=MESH,
        )

    def go_left(d):
        block = mode + d
        return pltpu.make_async_remote_copy(
            src_ref=basis if d == 0 else gath.at[block], dst_ref=gath.at[block],
            send_sem=left_send.at[d], recv_sem=left_recv.at[d],
            device_id={"mode": mode - 1}, device_id_type=MESH,
        )

    def halo(side, g=0):
        return pltpu.make_async_remote_copy(
            src_ref=gath.at[end] if g else basis, dst_ref=ext[g].at[pl.ds(2 * nbr * side, nbr)],
            send_sem=halo_send.at[g, side], recv_sem=halo_recv.at[g, side],
            device_id={"edge": edge + 1 - 2 * side}, device_id_type=MESH,
        )

    def landed(dst, sem):
        pltpu.make_async_copy(dst, dst, sem).wait()

    @pl.when(has_after)
    def _():
        halo(0).start()

    @pl.when(has_before)
    def _():
        halo(1).start()

    @pl.when(has_right)
    def _():
        go_right(0).start()

    @pl.when(has_left)
    def _():
        go_left(0).start()

    for copy in own:
        copy.wait()

    def halo_landed(g):
        @pl.when(has_before)
        def _():
            landed(ext[g].at[pl.ds(0, nbr)], halo_recv.at[g, 0])

        @pl.when(has_after)
        def _():
            landed(ext[g].at[pl.ds(2 * nbr, nbr)], halo_recv.at[g, 1])

    halo_landed(0)
    first = edge * nbr - nbr

    def block_row(g, r, carry):
        if g == 0:
            mot_copy(r).wait()
        count = counts_ref[r]
        tiles = [
            ext[g][jnp.where(k < count, cols_ref[r, k] - first, 3 * nbr)] for k in range(nnz)
        ]
        rhs = jnp.concatenate(tiles, axis=0)
        at = pl.ds(pl.multiple_of(r * bs, bs), bs)
        for q in range(2):
            lhs = jnp.concatenate([mot[q, r, k] for k in range(nnz)], axis=1)
            product = jnp.dot(lhs, rhs, preferred_element_type=jnp.float32)
            work[g, at, q * cl:(q + 1) * cl] = product.astype(jnp.bfloat16)
        return carry

    lax.fori_loop(0, nbr, functools.partial(block_row, 0), 0)

    def mate_copy(h):
        return pltpu.make_async_remote_copy(
            src_ref=to_mate.at[h], dst_ref=from_mate.at[h],
            send_sem=mate_send.at[h], recv_sem=mate_recv.at[h],
            device_id={"edge": mate}, device_id_type=MESH,
        )

    def chip_copy(h):
        return pltpu.make_async_remote_copy(
            src_ref=to_chip.at[h], dst_ref=from_chip.at[chip],
            send_sem=chip_send.at[h], recv_sem=chip_recv.at[chip],
            device_id={"edge": 2 * h + core}, device_id_type=MESH,
        )

    def mate_copy_far():
        return pltpu.make_async_remote_copy(
            src_ref=to_mate_far, dst_ref=from_mate_far, send_sem=far_send.at[0], recv_sem=far_recv,
            device_id={"edge": mate}, device_id_type=MESH,
        )

    def end_copy(s):
        return pltpu.make_async_remote_copy(
            src_ref=to_end, dst_ref=from_helper.at[chip], send_sem=far_send.at[1], recv_sem=end_recv.at[chip],
            device_id={"edge": s, "mode": end}, device_id_type=MESH,
        )

    def shares_of(block):
        return [(k, block * per_block + k) for k in range(per_block)]

    def times_work(block, g):
        return lax.dot_general(
            gath[block].reshape(rows, cl), work[g], (((0,), (0,)), ((), ())), preferred_element_type=jnp.float32
        )

    def product_of(block):
        total = times_work(block, 0)
        for k, s in shares_of(block):
            h = lax.div(s, 2)
            part = total[k * share:(k + 1) * share]

            @pl.when(lax.rem(s, 2) != core)
            def _():
                to_mate[h] = part
                mate_copy(h).start()

            @pl.when(lax.rem(s, 2) == core)
            def _():
                mine[h] = part

        for k, s in shares_of(block):
            h = lax.div(s, 2)

            @pl.when(lax.rem(s, 2) == core)
            def _():
                landed(from_mate.at[h], mate_recv.at[h])

                @pl.when(h != chip)
                def _():
                    to_chip[h] = mine[h] + from_mate[h]
                    chip_copy(h).start()

    def product_for_end():
        total = times_work(far, 1)
        for k, s in shares_of(far):
            part = total[k * share:(k + 1) * share]

            @pl.when(lax.rem(s, 2) != core)
            def _():
                to_mate_far[...] = part
                mate_copy_far().start()

            @pl.when(lax.rem(s, 2) == core)
            def _():
                mine_far[...] = part

        for k, s in shares_of(far):
            @pl.when(lax.rem(s, 2) == core)
            def _():
                landed(from_mate_far, far_recv)
                to_end[...] = mine_far[...] + from_mate_far[...]
                end_copy(s).start()

    product_of(mode)
    end_own = pltpu.make_async_copy(gath.at[end], ext[1].at[pl.ds(nbr, nbr)], own_sem.at[2])
    for d in range(1, n_mode - 1):
        @pl.when(mode >= d)
        def _():
            landed(gath.at[mode - d], right_recv.at[d - 1])

            if d < n_mode - 2:
                @pl.when(has_right)
                def _():
                    go_right(d).start()

        @pl.when(mode + d < n_mode)
        def _():
            landed(gath.at[mode + d], left_recv.at[d - 1])

            if d < n_mode - 2:
                @pl.when(has_left)
                def _():
                    go_left(d).start()

        if d == 1:
            @pl.when(is_helper & has_after)
            def _():
                halo(0, 1).start()

            @pl.when(is_helper & has_before)
            def _():
                halo(1, 1).start()

            @pl.when(is_helper)
            def _():
                end_own.start()

        if d == n_mode - 2:
            @pl.when(is_helper)
            def _():
                product_for_end()

        @pl.when(mode >= d)
        def _():
            product_of(mode - d)

        @pl.when(mode + d < n_mode)
        def _():
            product_of(mode + d)

        if d == 1:
            @pl.when(is_helper)
            def _():
                end_own.wait()
                halo_landed(1)
                lax.fori_loop(0, nbr, functools.partial(block_row, 1), 0)

    def reduced_here(s):
        return jnp.logical_not(is_end & (lax.div(s, per_block) == far))

    def put(total):
        for q in range(2):
            out[q] = total[:, q * cl:(q + 1) * cl]

    @pl.when(reduced_here(edge))
    def _():
        total = mine[chip] + from_mate[chip]
        for step in range(1, n_chip):
            other = lax.rem(chip + step, n_chip)
            landed(from_chip.at[other], chip_recv.at[other])
            total = total + from_chip[other]
        put(total)

    @pl.when(jnp.logical_not(reduced_here(edge)))
    def _():
        for other in range(n_chip):
            landed(from_helper.at[other], end_recv.at[other])
        total = from_helper[0]
        for other in range(1, n_chip):
            total = total + from_helper[other]
        put(total)

    for side, there in ((0, has_after), (1, has_before)):
        @pl.when(there)
        def _():
            halo(side).wait_send()

        @pl.when(there & is_helper)
        def _():
            halo(side, 1).wait_send()

    for d in range(n_mode - 2):
        @pl.when(has_right & (mode >= d))
        def _():
            go_right(d).wait_send()

        @pl.when(has_left & (mode + d < n_mode))
        def _():
            go_left(d).wait_send()

    for h in range(n_chip):
        @pl.when(reduced_here(2 * h + 1 - core))
        def _():
            mate_copy(h).wait_send()

        @pl.when((h != chip) & reduced_here(2 * h + core))
        def _():
            chip_copy(h).wait_send()

    for k, s in shares_of(far):
        @pl.when(is_helper & (lax.rem(s, 2) != core))
        def _():
            mate_copy_far().wait_send()

        @pl.when(is_helper & (lax.rem(s, 2) == core))
        def _():
            end_copy(s).wait_send()


def per_device(n_edge, n_mode, basis, motional, block_cols, block_counts):
    rows, cl = basis.shape
    nbr, nnz = block_cols.shape
    bs = motional.shape[-1]
    share = cl * n_mode // n_edge
    n_chip = n_edge // 2
    part = (n_chip, share, 2 * cl)
    dma = pltpu.SemaphoreType.DMA
    return pl.pallas_call(
        functools.partial(kernel, n_edge, n_mode),
        out_shape=jax.ShapeDtypeStruct((2, share, cl), jnp.float32),
        in_specs=[
            pl.BlockSpec(memory_space=pltpu.SMEM),
            pl.BlockSpec(memory_space=pltpu.SMEM),
            pl.BlockSpec(memory_space=pl.ANY),
            pl.BlockSpec(memory_space=pl.ANY),
        ],
        out_specs=pl.BlockSpec(memory_space=pltpu.VMEM),
        scratch_shapes=[
            pltpu.VMEM((3 * nbr + 1, bs, cl), jnp.bfloat16),
            pltpu.VMEM((3 * nbr + 1, bs, cl), jnp.bfloat16),
            pltpu.VMEM((n_mode, nbr, bs, cl), jnp.bfloat16),
            pltpu.VMEM((2, nbr, nnz, bs, bs), jnp.bfloat16),
            pltpu.VMEM((2, rows, 2 * cl), jnp.bfloat16),
            pltpu.VMEM(part, jnp.float32),
            pltpu.VMEM(part, jnp.float32),
            pltpu.VMEM(part, jnp.float32),
            pltpu.VMEM(part, jnp.float32),
            pltpu.VMEM(part, jnp.float32),
            pltpu.VMEM(part[1:], jnp.float32),
            pltpu.VMEM(part[1:], jnp.float32),
            pltpu.VMEM(part[1:], jnp.float32),
            pltpu.VMEM(part[1:], jnp.float32),
            pltpu.VMEM(part, jnp.float32),
            dma((3,)),
            dma((nbr,)),
            dma((2, 2)),
            dma((2, 2)),
            dma((n_mode,)),
            dma((n_mode,)),
            dma((n_mode,)),
            dma((n_mode,)),
            dma((n_chip,)),
            dma((n_chip,)),
            dma((n_chip,)),
            dma((n_chip,)),
            dma((2,)),
            dma(()),
            dma((n_chip,)),
        ],
        compiler_params=pltpu.CompilerParams(
            collective_id=0, has_side_effects=True, vmem_limit_bytes=48 * 2**20
        ),
    )(block_cols, block_counts, basis.reshape(nbr, bs, cl), motional)


def solution(mesh):
    placed = (
        P(("geom", "edge"), "mode"),
        P("geom", "edge", None, None, None),
        P(("geom", "edge"), None),
        P(("geom", "edge")),
    )
    return jax.shard_map(
        functools.partial(per_device, mesh.shape["edge"], mesh.shape["mode"]),
        mesh=mesh, in_specs=placed, out_specs=P("geom", "edge", "mode"), check_vma=False,
    )
```

```python
import functools

import jax
import jax.numpy as jnp
from jax import lax
from jax.experimental import pallas as pl
from jax.experimental.pallas import tpu as pltpu
from jax.sharding import PartitionSpec as P

MESH = pl.DeviceIdType.MESH


def kernel(
    n_edge, n_mode,
    cols_ref, counts_ref, basis, motional, out,
    ext_own, ext_end, gath, mot, work, mine, to_mate, from_mate, to_chip, from_chip,
    mine_far, to_mate_far, from_mate_far, to_end, from_helper,
    own_sem, mot_sem, halo_send, halo_recv, right_send, right_recv, left_send, left_recv,
    mate_send, mate_recv, chip_send, chip_recv, far_send, far_recv, end_recv,
):
    ext = (ext_own, ext_end)
    edge, mode = lax.axis_index("edge"), lax.axis_index("mode")
    nbr, bs, cl = basis.shape
    nnz = mot.shape[2]
    rows = nbr * bs
    n_chip = n_edge // 2
    share = mine.shape[1]
    per_block = cl // share
    chip, core = lax.div(edge, 2), lax.rem(edge, 2)
    mate = edge + 1 - 2 * core
    is_end = (mode == 0) | (mode == n_mode - 1)
    is_helper = (mode == 1) | (mode == n_mode - 2)
    low = (mode < 2).astype(jnp.int32)
    end = (n_mode - 1) * (1 - low)
    far = (n_mode - 1) * low
    helper = end + 2 * low - 1

    barrier = pltpu.get_barrier_semaphore()
    for step in range(1, n_edge):
        pl.semaphore_signal(barrier, inc=1, device_id={"edge": lax.rem(edge + step, n_edge)}, device_id_type=MESH)
    has_left, has_right = mode > 0, mode < n_mode - 1
    has_before, has_after = edge > 0, edge < n_edge - 1

    @pl.when(has_left)
    def _():
        pl.semaphore_signal(barrier, inc=1, device_id={"mode": mode - 1}, device_id_type=MESH)

    @pl.when(has_right)
    def _():
        pl.semaphore_signal(barrier, inc=1, device_id={"mode": mode + 1}, device_id_type=MESH)

    for step in range(1, n_edge):
        to = lax.rem(edge + step, n_edge)

        @pl.when(is_end)
        def _():
            pl.semaphore_signal(barrier, inc=1, device_id={"edge": to, "mode": helper}, device_id_type=MESH)

        @pl.when(is_helper)
        def _():
            pl.semaphore_signal(barrier, inc=1, device_id={"edge": to, "mode": end}, device_id_type=MESH)

    own = [
        pltpu.make_async_copy(basis, ext[0].at[pl.ds(nbr, nbr)], own_sem.at[0]),
        pltpu.make_async_copy(basis, gath.at[mode], own_sem.at[1]),
    ]

    def mot_copy(r):
        return pltpu.make_async_copy(motional.at[:, r], mot.at[:, r], mot_sem.at[r])

    for copy in own:
        copy.start()
    for r in range(nbr):
        mot_copy(r).start()
    for g in range(2):
        ext[g][3 * nbr] = jnp.zeros((bs, cl), jnp.bfloat16)

    crossing = (n_edge - 1) * (is_end | is_helper).astype(jnp.int32)
    pl.semaphore_wait(barrier, n_edge - 1 + has_left.astype(jnp.int32) + has_right.astype(jnp.int32) + crossing)

    def go_right(d):
        block = mode - d
        return pltpu.make_async_remote_copy(
            src_ref=basis if d == 0 else gath.at[block], dst_ref=gath.at[block],
            send_sem=right_send.at[d], recv_sem=right_recv.at[d],
            device_id={"mode": mode + 1}, device_id_type=MESH,
        )

    def go_left(d):
        block = mode + d
        return pltpu.make_async_remote_copy(
            src_ref=basis if d == 0 else gath.at[block], dst_ref=gath.at[block],
            send_sem=left_send.at[d], recv_sem=left_recv.at[d],
            device_id={"mode": mode - 1}, device_id_type=MESH,
        )

    def halo(side, g=0):
        return pltpu.make_async_remote_copy(
            src_ref=gath.at[end] if g else basis, dst_ref=ext[g].at[pl.ds(2 * nbr * side, nbr)],
            send_sem=halo_send.at[g, side], recv_sem=halo_recv.at[g, side],
            device_id={"edge": edge + 1 - 2 * side}, device_id_type=MESH,
        )

    def landed(dst, sem):
        pltpu.make_async_copy(dst, dst, sem).wait()

    @pl.when(has_after)
    def _():
        halo(0).start()

    @pl.when(has_before)
    def _():
        halo(1).start()

    @pl.when(has_right)
    def _():
        go_right(0).start()

    @pl.when(has_left)
    def _():
        go_left(0).start()

    for copy in own:
        copy.wait()

    def halo_landed(g):
        @pl.when(has_before)
        def _():
            landed(ext[g].at[pl.ds(0, nbr)], halo_recv.at[g, 0])

        @pl.when(has_after)
        def _():
            landed(ext[g].at[pl.ds(2 * nbr, nbr)], halo_recv.at[g, 1])

    halo_landed(0)
    first = edge * nbr - nbr

    def block_row(g, r, carry):
        if g == 0:
            mot_copy(r).wait()
        count = counts_ref[r]
        tiles = [
            ext[g][jnp.where(k < count, cols_ref[r, k] - first, 3 * nbr)] for k in range(nnz)
        ]
        rhs = jnp.concatenate(tiles, axis=0)
        at = pl.ds(pl.multiple_of(r * bs, bs), bs)
        for q in range(2):
            lhs = jnp.concatenate([mot[q, r, k] for k in range(nnz)], axis=1)
            product = jnp.dot(lhs, rhs, preferred_element_type=jnp.float32)
            work[g, at, q * cl:(q + 1) * cl] = product.astype(jnp.bfloat16)
        return carry

    lax.fori_loop(0, nbr, functools.partial(block_row, 0), 0)

    def mate_copy(h):
        return pltpu.make_async_remote_copy(
            src_ref=to_mate.at[h], dst_ref=from_mate.at[h],
            send_sem=mate_send.at[h], recv_sem=mate_recv.at[h],
            device_id={"edge": mate}, device_id_type=MESH,
        )

    def chip_copy(h):
        return pltpu.make_async_remote_copy(
            src_ref=to_chip.at[h], dst_ref=from_chip.at[chip],
            send_sem=chip_send.at[h], recv_sem=chip_recv.at[chip],
            device_id={"edge": 2 * h + core}, device_id_type=MESH,
        )

    def mate_copy_far():
        return pltpu.make_async_remote_copy(
            src_ref=to_mate_far, dst_ref=from_mate_far, send_sem=far_send.at[0], recv_sem=far_recv,
            device_id={"edge": mate}, device_id_type=MESH,
        )

    def end_copy(s):
        return pltpu.make_async_remote_copy(
            src_ref=to_end, dst_ref=from_helper.at[chip], send_sem=far_send.at[1], recv_sem=end_recv.at[chip],
            device_id={"edge": s, "mode": end}, device_id_type=MESH,
        )

    def shares_of(block):
        return [(k, block * per_block + k) for k in range(per_block)]

    def times_work(block, g):
        return lax.dot_general(
            gath[block].reshape(rows, cl), work[g], (((0,), (0,)), ((), ())), preferred_element_type=jnp.float32
        )

    def product_of(block):
        total = times_work(block, 0)
        for k, s in shares_of(block):
            h = lax.div(s, 2)
            part = total[k * share:(k + 1) * share]

            @pl.when(lax.rem(s, 2) != core)
            def _():
                to_mate[h] = part
                mate_copy(h).start()

            @pl.when(lax.rem(s, 2) == core)
            def _():
                mine[h] = part

        for k, s in shares_of(block):
            h = lax.div(s, 2)

            @pl.when(lax.rem(s, 2) == core)
            def _():
                landed(from_mate.at[h], mate_recv.at[h])

                @pl.when(h != chip)
                def _():
                    to_chip[h] = (mine[h] + from_mate[h]).astype(to_chip.dtype)
                    chip_copy(h).start()

    def product_for_end():
        total = times_work(far, 1)
        for k, s in shares_of(far):
            part = total[k * share:(k + 1) * share]

            @pl.when(lax.rem(s, 2) != core)
            def _():
                to_mate_far[...] = part
                mate_copy_far().start()

            @pl.when(lax.rem(s, 2) == core)
            def _():
                mine_far[...] = part

        for k, s in shares_of(far):
            @pl.when(lax.rem(s, 2) == core)
            def _():
                landed(from_mate_far, far_recv)
                to_end[...] = (mine_far[...] + from_mate_far[...]).astype(to_end.dtype)
                end_copy(s).start()

    product_of(mode)
    end_own = pltpu.make_async_copy(gath.at[end], ext[1].at[pl.ds(nbr, nbr)], own_sem.at[2])
    for d in range(1, n_mode - 1):
        @pl.when(mode >= d)
        def _():
            landed(gath.at[mode - d], right_recv.at[d - 1])

            if d < n_mode - 2:
                @pl.when(has_right)
                def _():
                    go_right(d).start()

        @pl.when(mode + d < n_mode)
        def _():
            landed(gath.at[mode + d], left_recv.at[d - 1])

            if d < n_mode - 2:
                @pl.when(has_left)
                def _():
                    go_left(d).start()

        if d == 1:
            @pl.when(is_helper & has_after)
            def _():
                halo(0, 1).start()

            @pl.when(is_helper & has_before)
            def _():
                halo(1, 1).start()

            @pl.when(is_helper)
            def _():
                end_own.start()

        if d == n_mode - 2:
            @pl.when(is_helper)
            def _():
                product_for_end()

        @pl.when(mode >= d)
        def _():
            product_of(mode - d)

        @pl.when(mode + d < n_mode)
        def _():
            product_of(mode + d)

        if d == 1:
            @pl.when(is_helper)
            def _():
                end_own.wait()
                halo_landed(1)
                lax.fori_loop(0, nbr, functools.partial(block_row, 1), 0)

    def reduced_here(s):
        return jnp.logical_not(is_end & (lax.div(s, per_block) == far))

    def put(total):
        for q in range(2):
            out[q] = total[:, q * cl:(q + 1) * cl]

    @pl.when(reduced_here(edge))
    def _():
        total = mine[chip] + from_mate[chip]
        for step in range(1, n_chip):
            other = lax.rem(chip + step, n_chip)
            landed(from_chip.at[other], chip_recv.at[other])
            total = total + from_chip[other].astype(jnp.float32)
        put(total)

    @pl.when(jnp.logical_not(reduced_here(edge)))
    def _():
        for other in range(n_chip):
            landed(from_helper.at[other], end_recv.at[other])
        total = from_helper[0].astype(jnp.float32)
        for other in range(1, n_chip):
            total = total + from_helper[other].astype(jnp.float32)
        put(total)

    for side, there in ((0, has_after), (1, has_before)):
        @pl.when(there)
        def _():
            halo(side).wait_send()

        @pl.when(there & is_helper)
        def _():
            halo(side, 1).wait_send()

    for d in range(n_mode - 2):
        @pl.when(has_right & (mode >= d))
        def _():
            go_right(d).wait_send()

        @pl.when(has_left & (mode + d < n_mode))
        def _():
            go_left(d).wait_send()

    for h in range(n_chip):
        @pl.when(reduced_here(2 * h + 1 - core))
        def _():
            mate_copy(h).wait_send()

        @pl.when((h != chip) & reduced_here(2 * h + core))
        def _():
            chip_copy(h).wait_send()

    for k, s in shares_of(far):
        @pl.when(is_helper & (lax.rem(s, 2) != core))
        def _():
            mate_copy_far().wait_send()

        @pl.when(is_helper & (lax.rem(s, 2) == core))
        def _():
            end_copy(s).wait_send()


def per_device(n_edge, n_mode, basis, motional, block_cols, block_counts):
    rows, cl = basis.shape
    nbr, nnz = block_cols.shape
    bs = motional.shape[-1]
    share = cl * n_mode // n_edge
    n_chip = n_edge // 2
    part = (n_chip, share, 2 * cl)
    dma = pltpu.SemaphoreType.DMA
    return pl.pallas_call(
        functools.partial(kernel, n_edge, n_mode),
        out_shape=jax.ShapeDtypeStruct((2, share, cl), jnp.float32),
        in_specs=[
            pl.BlockSpec(memory_space=pltpu.SMEM),
            pl.BlockSpec(memory_space=pltpu.SMEM),
            pl.BlockSpec(memory_space=pl.ANY),
            pl.BlockSpec(memory_space=pl.ANY),
        ],
        out_specs=pl.BlockSpec(memory_space=pltpu.VMEM),
        scratch_shapes=[
            pltpu.VMEM((3 * nbr + 1, bs, cl), jnp.bfloat16),
            pltpu.VMEM((3 * nbr + 1, bs, cl), jnp.bfloat16),
            pltpu.VMEM((n_mode, nbr, bs, cl), jnp.bfloat16),
            pltpu.VMEM((2, nbr, nnz, bs, bs), jnp.bfloat16),
            pltpu.VMEM((2, rows, 2 * cl), jnp.bfloat16),
            pltpu.VMEM(part, jnp.float32),
            pltpu.VMEM(part, jnp.float32),
            pltpu.VMEM(part, jnp.float32),
            pltpu.VMEM(part, jnp.bfloat16),
            pltpu.VMEM(part, jnp.bfloat16),
            pltpu.VMEM(part[1:], jnp.float32),
            pltpu.VMEM(part[1:], jnp.float32),
            pltpu.VMEM(part[1:], jnp.float32),
            pltpu.VMEM(part[1:], jnp.bfloat16),
            pltpu.VMEM(part, jnp.bfloat16),
            dma((3,)),
            dma((nbr,)),
            dma((2, 2)),
            dma((2, 2)),
            dma((n_mode,)),
            dma((n_mode,)),
            dma((n_mode,)),
            dma((n_mode,)),
            dma((n_chip,)),
            dma((n_chip,)),
            dma((n_chip,)),
            dma((n_chip,)),
            dma((2,)),
            dma(()),
            dma((n_chip,)),
        ],
        compiler_params=pltpu.CompilerParams(
            collective_id=0, has_side_effects=True, vmem_limit_bytes=60 * 2**20
        ),
    )(block_cols, block_counts, basis.reshape(nbr, bs, cl), motional)


def solution(mesh):
    placed = (
        P(("geom", "edge"), "mode"),
        P("geom", "edge", None, None, None),
        P(("geom", "edge"), None),
        P(("geom", "edge")),
    )
    return jax.shard_map(
        functools.partial(per_device, mesh.shape["edge"], mesh.shape["mode"]),
        mesh=mesh, in_specs=placed, out_specs=P("geom", "edge", "mode"), check_vma=False,
    )
```

```python
import functools

import jax
import jax.numpy as jnp
from jax import lax
from jax.experimental import pallas as pl
from jax.experimental.pallas import tpu as pltpu
from jax.sharding import PartitionSpec as P

MESH = pl.DeviceIdType.MESH


def kernel(
    n_edge, n_mode,
    cols_ref, counts_ref, basis, motional, out,
    ext_own, ext_end, gath, mot, work, mine, to_mate, from_mate, to_chip, from_chip,
    mine_far, to_mate_far, from_mate_far, to_end, from_helper,
    own_sem, mot_sem, halo_send, halo_recv, right_send, right_recv, left_send, left_recv,
    mate_send, mate_recv, chip_send, chip_recv, far_send, far_recv, end_recv,
):
    ext = (ext_own, ext_end)
    edge, mode = lax.axis_index("edge"), lax.axis_index("mode")
    nbr, bs, cl = basis.shape
    nnz = mot.shape[2]
    rows = nbr * bs
    n_chip = n_edge // 2
    share = mine.shape[2]
    per_block = cl // share
    chip, core = lax.div(edge, 2), lax.rem(edge, 2)
    mate = edge + 1 - 2 * core
    is_end = (mode == 0) | (mode == n_mode - 1)
    is_helper = (mode == 1) | (mode == n_mode - 2)
    low = (mode < 2).astype(jnp.int32)
    end = (n_mode - 1) * (1 - low)
    far = (n_mode - 1) * low
    helper = end + 2 * low - 1

    barrier = pltpu.get_barrier_semaphore()
    for step in range(1, n_edge):
        pl.semaphore_signal(barrier, inc=1, device_id={"edge": lax.rem(edge + step, n_edge)}, device_id_type=MESH)
    has_left, has_right = mode > 0, mode < n_mode - 1
    has_before, has_after = edge > 0, edge < n_edge - 1

    @pl.when(has_left)
    def _():
        pl.semaphore_signal(barrier, inc=1, device_id={"mode": mode - 1}, device_id_type=MESH)

    @pl.when(has_right)
    def _():
        pl.semaphore_signal(barrier, inc=1, device_id={"mode": mode + 1}, device_id_type=MESH)

    for step in range(1, n_edge):
        to = lax.rem(edge + step, n_edge)

        @pl.when(is_end)
        def _():
            pl.semaphore_signal(barrier, inc=1, device_id={"edge": to, "mode": helper}, device_id_type=MESH)

        @pl.when(is_helper)
        def _():
            pl.semaphore_signal(barrier, inc=1, device_id={"edge": to, "mode": end}, device_id_type=MESH)

    own = [
        pltpu.make_async_copy(basis, ext[0].at[pl.ds(nbr, nbr)], own_sem.at[0]),
        pltpu.make_async_copy(basis, gath.at[mode], own_sem.at[1]),
    ]

    def mot_copy(r):
        return pltpu.make_async_copy(motional.at[:, r], mot.at[:, r], mot_sem.at[r])

    for copy in own:
        copy.start()
    for r in range(nbr):
        mot_copy(r).start()
    for g in range(2):
        ext[g][3 * nbr] = jnp.zeros((bs, cl), jnp.bfloat16)

    crossing = (n_edge - 1) * (is_end | is_helper).astype(jnp.int32)
    pl.semaphore_wait(barrier, n_edge - 1 + has_left.astype(jnp.int32) + has_right.astype(jnp.int32) + crossing)

    def go_right(d):
        block = mode - d
        return pltpu.make_async_remote_copy(
            src_ref=basis if d == 0 else gath.at[block], dst_ref=gath.at[block],
            send_sem=right_send.at[d], recv_sem=right_recv.at[d],
            device_id={"mode": mode + 1}, device_id_type=MESH,
        )

    def go_left(d):
        block = mode + d
        return pltpu.make_async_remote_copy(
            src_ref=basis if d == 0 else gath.at[block], dst_ref=gath.at[block],
            send_sem=left_send.at[d], recv_sem=left_recv.at[d],
            device_id={"mode": mode - 1}, device_id_type=MESH,
        )

    def halo(side, g=0):
        return pltpu.make_async_remote_copy(
            src_ref=gath.at[end] if g else basis, dst_ref=ext[g].at[pl.ds(2 * nbr * side, nbr)],
            send_sem=halo_send.at[g, side], recv_sem=halo_recv.at[g, side],
            device_id={"edge": edge + 1 - 2 * side}, device_id_type=MESH,
        )

    def landed(dst, sem):
        pltpu.make_async_copy(dst, dst, sem).wait()

    @pl.when(has_after)
    def _():
        halo(0).start()

    @pl.when(has_before)
    def _():
        halo(1).start()

    @pl.when(has_right)
    def _():
        go_right(0).start()

    @pl.when(has_left)
    def _():
        go_left(0).start()

    for copy in own:
        copy.wait()

    def halo_landed(g):
        @pl.when(has_before)
        def _():
            landed(ext[g].at[pl.ds(0, nbr)], halo_recv.at[g, 0])

        @pl.when(has_after)
        def _():
            landed(ext[g].at[pl.ds(2 * nbr, nbr)], halo_recv.at[g, 1])

    halo_landed(0)
    first = edge * nbr - nbr

    def block_row(g, r, carry):
        if g == 0:
            mot_copy(r).wait()
        count = counts_ref[r]
        tiles = [
            ext[g][jnp.where(k < count, cols_ref[r, k] - first, 3 * nbr)] for k in range(nnz)
        ]
        rhs = jnp.concatenate(tiles, axis=0)
        at = pl.ds(pl.multiple_of(r * bs, bs), bs)
        for q in range(2):
            lhs = jnp.concatenate([mot[q, r, k] for k in range(nnz)], axis=1)
            product = jnp.dot(lhs, rhs, preferred_element_type=jnp.float32)
            work[g, at, q * cl:(q + 1) * cl] = product.astype(jnp.bfloat16)
        return carry

    lax.fori_loop(0, nbr, functools.partial(block_row, 0), 0)

    def mate_copy(h, q):
        return pltpu.make_async_remote_copy(
            src_ref=to_mate.at[h, q], dst_ref=from_mate.at[h, q],
            send_sem=mate_send.at[h, q], recv_sem=mate_recv.at[h, q],
            device_id={"edge": mate}, device_id_type=MESH,
        )

    def chip_copy(h, q):
        return pltpu.make_async_remote_copy(
            src_ref=to_chip.at[h, q], dst_ref=from_chip.at[chip, q],
            send_sem=chip_send.at[h, q], recv_sem=chip_recv.at[chip, q],
            device_id={"edge": 2 * h + core}, device_id_type=MESH,
        )

    def mate_copy_far(q):
        return pltpu.make_async_remote_copy(
            src_ref=to_mate_far.at[q], dst_ref=from_mate_far.at[q],
            send_sem=far_send.at[0, q], recv_sem=far_recv.at[q],
            device_id={"edge": mate}, device_id_type=MESH,
        )

    def end_copy(s, q):
        return pltpu.make_async_remote_copy(
            src_ref=to_end.at[q], dst_ref=from_helper.at[chip, q],
            send_sem=far_send.at[1, q], recv_sem=end_recv.at[chip, q],
            device_id={"edge": s, "mode": end}, device_id_type=MESH,
        )

    def shares_of(block):
        return [(k, block * per_block + k) for k in range(per_block)]

    def times_work(block, g, q):
        return lax.dot_general(
            gath[block].reshape(rows, cl), work[g, :, q * cl:(q + 1) * cl], (((0,), (0,)), ((), ())),
            preferred_element_type=jnp.float32,
        )

    def product_of(block):
        for q in range(2):
            total = times_work(block, 0, q)
            for k, s in shares_of(block):
                h = lax.div(s, 2)
                part = total[k * share:(k + 1) * share]

                @pl.when(lax.rem(s, 2) != core)
                def _():
                    to_mate[h, q] = part
                    mate_copy(h, q).start()

                @pl.when(lax.rem(s, 2) == core)
                def _():
                    mine[h, q] = part

        for k, s in shares_of(block):
            h = lax.div(s, 2)

            @pl.when(lax.rem(s, 2) == core)
            def _():
                for q in range(2):
                    landed(from_mate.at[h, q], mate_recv.at[h, q])

                    @pl.when(h != chip)
                    def _():
                        to_chip[h, q] = (mine[h, q] + from_mate[h, q]).astype(to_chip.dtype)
                        chip_copy(h, q).start()

    def product_for_end():
        for q in range(2):
            total = times_work(far, 1, q)
            for k, s in shares_of(far):
                part = total[k * share:(k + 1) * share]

                @pl.when(lax.rem(s, 2) != core)
                def _():
                    to_mate_far[q] = part
                    mate_copy_far(q).start()

                @pl.when(lax.rem(s, 2) == core)
                def _():
                    mine_far[q] = part

        for k, s in shares_of(far):
            @pl.when(lax.rem(s, 2) == core)
            def _():
                for q in range(2):
                    landed(from_mate_far.at[q], far_recv.at[q])
                    to_end[q] = (mine_far[q] + from_mate_far[q]).astype(to_end.dtype)
                    end_copy(s, q).start()

    product_of(mode)
    end_own = pltpu.make_async_copy(gath.at[end], ext[1].at[pl.ds(nbr, nbr)], own_sem.at[2])
    for d in range(1, n_mode - 1):
        @pl.when(mode >= d)
        def _():
            landed(gath.at[mode - d], right_recv.at[d - 1])

            if d < n_mode - 2:
                @pl.when(has_right)
                def _():
                    go_right(d).start()

        @pl.when(mode + d < n_mode)
        def _():
            landed(gath.at[mode + d], left_recv.at[d - 1])

            if d < n_mode - 2:
                @pl.when(has_left)
                def _():
                    go_left(d).start()

        if d == 1:
            @pl.when(is_helper & has_after)
            def _():
                halo(0, 1).start()

            @pl.when(is_helper & has_before)
            def _():
                halo(1, 1).start()

            @pl.when(is_helper)
            def _():
                end_own.start()

        if d == n_mode - 2:
            @pl.when(is_helper)
            def _():
                product_for_end()

        @pl.when(mode >= d)
        def _():
            product_of(mode - d)

        @pl.when(mode + d < n_mode)
        def _():
            product_of(mode + d)

        if d == 1:
            @pl.when(is_helper)
            def _():
                end_own.wait()
                halo_landed(1)
                lax.fori_loop(0, nbr, functools.partial(block_row, 1), 0)

    def reduced_here(s):
        return jnp.logical_not(is_end & (lax.div(s, per_block) == far))

    @pl.when(reduced_here(edge))
    def _():
        for q in range(2):
            total = mine[chip, q] + from_mate[chip, q]
            for step in range(1, n_chip):
                other = lax.rem(chip + step, n_chip)
                landed(from_chip.at[other, q], chip_recv.at[other, q])
                total = total + from_chip[other, q].astype(jnp.float32)
            out[q] = total

    @pl.when(jnp.logical_not(reduced_here(edge)))
    def _():
        for q in range(2):
            total = jnp.zeros((share, cl), jnp.float32)
            for other in range(n_chip):
                landed(from_helper.at[other, q], end_recv.at[other, q])
                total = total + from_helper[other, q].astype(jnp.float32)
            out[q] = total

    for side, there in ((0, has_after), (1, has_before)):
        @pl.when(there)
        def _():
            halo(side).wait_send()

        @pl.when(there & is_helper)
        def _():
            halo(side, 1).wait_send()

    for d in range(n_mode - 2):
        @pl.when(has_right & (mode >= d))
        def _():
            go_right(d).wait_send()

        @pl.when(has_left & (mode + d < n_mode))
        def _():
            go_left(d).wait_send()

    for h in range(n_chip):
        @pl.when(reduced_here(2 * h + 1 - core))
        def _():
            for q in range(2):
                mate_copy(h, q).wait_send()

        @pl.when((h != chip) & reduced_here(2 * h + core))
        def _():
            for q in range(2):
                chip_copy(h, q).wait_send()

    for k, s in shares_of(far):
        @pl.when(is_helper & (lax.rem(s, 2) != core))
        def _():
            for q in range(2):
                mate_copy_far(q).wait_send()

        @pl.when(is_helper & (lax.rem(s, 2) == core))
        def _():
            for q in range(2):
                end_copy(s, q).wait_send()


def per_device(n_edge, n_mode, basis, motional, block_cols, block_counts):
    rows, cl = basis.shape
    nbr, nnz = block_cols.shape
    bs = motional.shape[-1]
    share = cl * n_mode // n_edge
    n_chip = n_edge // 2
    part = (n_chip, 2, share, cl)
    dma = pltpu.SemaphoreType.DMA
    return pl.pallas_call(
        functools.partial(kernel, n_edge, n_mode),
        out_shape=jax.ShapeDtypeStruct((2, share, cl), jnp.float32),
        in_specs=[
            pl.BlockSpec(memory_space=pltpu.SMEM),
            pl.BlockSpec(memory_space=pltpu.SMEM),
            pl.BlockSpec(memory_space=pl.ANY),
            pl.BlockSpec(memory_space=pl.ANY),
        ],
        out_specs=pl.BlockSpec(memory_space=pltpu.VMEM),
        scratch_shapes=[
            pltpu.VMEM((3 * nbr + 1, bs, cl), jnp.bfloat16),
            pltpu.VMEM((3 * nbr + 1, bs, cl), jnp.bfloat16),
            pltpu.VMEM((n_mode, nbr, bs, cl), jnp.bfloat16),
            pltpu.VMEM((2, nbr, nnz, bs, bs), jnp.bfloat16),
            pltpu.VMEM((2, rows, 2 * cl), jnp.bfloat16),
            pltpu.VMEM(part, jnp.float32),
            pltpu.VMEM(part, jnp.float32),
            pltpu.VMEM(part, jnp.float32),
            pltpu.VMEM(part, jnp.bfloat16),
            pltpu.VMEM(part, jnp.bfloat16),
            pltpu.VMEM(part[1:], jnp.float32),
            pltpu.VMEM(part[1:], jnp.float32),
            pltpu.VMEM(part[1:], jnp.float32),
            pltpu.VMEM(part[1:], jnp.bfloat16),
            pltpu.VMEM(part, jnp.bfloat16),
            dma((3,)),
            dma((nbr,)),
            dma((2, 2)),
            dma((2, 2)),
            dma((n_mode,)),
            dma((n_mode,)),
            dma((n_mode,)),
            dma((n_mode,)),
            dma((n_chip, 2)),
            dma((n_chip, 2)),
            dma((n_chip, 2)),
            dma((n_chip, 2)),
            dma((2, 2)),
            dma((2,)),
            dma((n_chip, 2)),
        ],
        compiler_params=pltpu.CompilerParams(
            collective_id=0, has_side_effects=True, vmem_limit_bytes=60 * 2**20
        ),
    )(block_cols, block_counts, basis.reshape(nbr, bs, cl), motional)


def solution(mesh):
    placed = (
        P(("geom", "edge"), "mode"),
        P("geom", "edge", None, None, None),
        P(("geom", "edge"), None),
        P(("geom", "edge")),
    )
    return jax.shard_map(
        functools.partial(per_device, mesh.shape["edge"], mesh.shape["mode"]),
        mesh=mesh, in_specs=placed, out_specs=P("geom", "edge", "mode"), check_vma=False,
    )
```

```python
import functools

import jax
import jax.numpy as jnp
from jax import lax
from jax.experimental import pallas as pl
from jax.experimental.pallas import tpu as pltpu
from jax.sharding import PartitionSpec as P

MESH = pl.DeviceIdType.MESH


def kernel(
    n_edge, n_mode,
    cols_ref, counts_ref, basis, motional, out,
    ext_own, ext_end, gath, mot, work, mine, to_mate, from_mate, to_chip, from_chip,
    mine_far, to_mate_far, from_mate_far, to_end, from_helper,
    own_sem, mot_sem, halo_send, halo_recv, right_send, right_recv, left_send, left_recv,
    mate_send, mate_recv, chip_send, chip_recv, far_send, far_recv, end_recv,
):
    ext = (ext_own, ext_end)
    edge, mode = lax.axis_index("edge"), lax.axis_index("mode")
    nbr, bs, cl = basis.shape
    nnz = mot.shape[2]
    rows = nbr * bs
    n_chip = n_edge // 2
    share = mine.shape[1]
    per_block = cl // share
    chip, core = lax.div(edge, 2), lax.rem(edge, 2)
    mate = edge + 1 - 2 * core
    is_end = (mode == 0) | (mode == n_mode - 1)
    is_helper = (mode == 1) | (mode == n_mode - 2)
    low = (mode < 2).astype(jnp.int32)
    end = (n_mode - 1) * (1 - low)
    far = (n_mode - 1) * low
    helper = end + 2 * low - 1

    barrier = pltpu.get_barrier_semaphore()
    for step in range(1, n_edge):
        pl.semaphore_signal(barrier, inc=1, device_id={"edge": lax.rem(edge + step, n_edge)}, device_id_type=MESH)
    has_left, has_right = mode > 0, mode < n_mode - 1
    has_before, has_after = edge > 0, edge < n_edge - 1

    @pl.when(has_left)
    def _():
        pl.semaphore_signal(barrier, inc=1, device_id={"mode": mode - 1}, device_id_type=MESH)

    @pl.when(has_right)
    def _():
        pl.semaphore_signal(barrier, inc=1, device_id={"mode": mode + 1}, device_id_type=MESH)

    for step in range(1, n_edge):
        to = lax.rem(edge + step, n_edge)

        @pl.when(is_end)
        def _():
            pl.semaphore_signal(barrier, inc=1, device_id={"edge": to, "mode": helper}, device_id_type=MESH)

        @pl.when(is_helper)
        def _():
            pl.semaphore_signal(barrier, inc=1, device_id={"edge": to, "mode": end}, device_id_type=MESH)

    own = [
        pltpu.make_async_copy(basis, ext[0].at[pl.ds(nbr, nbr)], own_sem.at[0]),
        pltpu.make_async_copy(basis, gath.at[mode], own_sem.at[1]),
    ]

    def mot_copy(r):
        return pltpu.make_async_copy(motional.at[:, r], mot.at[:, r], mot_sem.at[r])

    for copy in own:
        copy.start()
    for r in range(nbr):
        mot_copy(r).start()
    for g in range(2):
        ext[g][3 * nbr] = jnp.zeros((bs, cl), jnp.bfloat16)

    crossing = (n_edge - 1) * (is_end | is_helper).astype(jnp.int32)
    pl.semaphore_wait(barrier, n_edge - 1 + has_left.astype(jnp.int32) + has_right.astype(jnp.int32) + crossing)

    def half(c):
        return pl.ds(c * (nbr // 2), nbr // 2)

    def go_right(d, c):
        block = mode - d
        return pltpu.make_async_remote_copy(
            src_ref=basis.at[half(c)] if d == 0 else gath.at[block, half(c)], dst_ref=gath.at[block, half(c)],
            send_sem=right_send.at[d, c], recv_sem=right_recv.at[d, c],
            device_id={"mode": mode + 1}, device_id_type=MESH,
        )

    def go_left(d, c):
        block = mode + d
        return pltpu.make_async_remote_copy(
            src_ref=basis.at[half(c)] if d == 0 else gath.at[block, half(c)], dst_ref=gath.at[block, half(c)],
            send_sem=left_send.at[d, c], recv_sem=left_recv.at[d, c],
            device_id={"mode": mode - 1}, device_id_type=MESH,
        )

    def halo(side, g=0):
        return pltpu.make_async_remote_copy(
            src_ref=gath.at[end] if g else basis, dst_ref=ext[g].at[pl.ds(2 * nbr * side, nbr)],
            send_sem=halo_send.at[g, side], recv_sem=halo_recv.at[g, side],
            device_id={"edge": edge + 1 - 2 * side}, device_id_type=MESH,
        )

    def landed(dst, sem):
        pltpu.make_async_copy(dst, dst, sem).wait()

    @pl.when(has_after)
    def _():
        halo(0).start()

    @pl.when(has_before)
    def _():
        halo(1).start()

    for c in range(2):
        @pl.when(has_right)
        def _():
            go_right(0, c).start()

        @pl.when(has_left)
        def _():
            go_left(0, c).start()

    def pass_on(d, c):
        @pl.when(mode >= d)
        def _():
            landed(gath.at[mode - d, half(c)], right_recv.at[d - 1, c])

            if d < n_mode - 2:
                @pl.when(has_right)
                def _():
                    go_right(d, c).start()

        @pl.when(mode + d < n_mode)
        def _():
            landed(gath.at[mode + d, half(c)], left_recv.at[d - 1, c])

            if d < n_mode - 2:
                @pl.when(has_left)
                def _():
                    go_left(d, c).start()

    for copy in own:
        copy.wait()

    def halo_landed(g):
        @pl.when(has_before)
        def _():
            landed(ext[g].at[pl.ds(0, nbr)], halo_recv.at[g, 0])

        @pl.when(has_after)
        def _():
            landed(ext[g].at[pl.ds(2 * nbr, nbr)], halo_recv.at[g, 1])

    halo_landed(0)
    first = edge * nbr - nbr

    def block_row(g, r, carry):
        if g == 0:
            mot_copy(r).wait()
        count = counts_ref[r]
        tiles = [
            ext[g][jnp.where(k < count, cols_ref[r, k] - first, 3 * nbr)] for k in range(nnz)
        ]
        rhs = jnp.concatenate(tiles, axis=0)
        at = pl.ds(pl.multiple_of(r * bs, bs), bs)
        for q in range(2):
            lhs = jnp.concatenate([mot[q, r, k] for k in range(nnz)], axis=1)
            product = jnp.dot(lhs, rhs, preferred_element_type=jnp.float32)
            work[g, at, q * cl:(q + 1) * cl] = product.astype(jnp.bfloat16)
        return carry

    lax.fori_loop(0, nbr // 2, functools.partial(block_row, 0), 0)
    pass_on(1, 0)
    lax.fori_loop(nbr // 2, nbr, functools.partial(block_row, 0), 0)
    pass_on(1, 1)

    def mate_copy(h):
        return pltpu.make_async_remote_copy(
            src_ref=to_mate.at[h], dst_ref=from_mate.at[h],
            send_sem=mate_send.at[h], recv_sem=mate_recv.at[h],
            device_id={"edge": mate}, device_id_type=MESH,
        )

    def chip_copy(h):
        return pltpu.make_async_remote_copy(
            src_ref=to_chip.at[h], dst_ref=from_chip.at[chip],
            send_sem=chip_send.at[h], recv_sem=chip_recv.at[chip],
            device_id={"edge": 2 * h + core}, device_id_type=MESH,
        )

    def mate_copy_far():
        return pltpu.make_async_remote_copy(
            src_ref=to_mate_far, dst_ref=from_mate_far, send_sem=far_send.at[0], recv_sem=far_recv,
            device_id={"edge": mate}, device_id_type=MESH,
        )

    def end_copy(s):
        return pltpu.make_async_remote_copy(
            src_ref=to_end, dst_ref=from_helper.at[chip], send_sem=far_send.at[1], recv_sem=end_recv.at[chip],
            device_id={"edge": s, "mode": end}, device_id_type=MESH,
        )

    def shares_of(block):
        return [(k, block * per_block + k) for k in range(per_block)]

    def times_work(block, g):
        return lax.dot_general(
            gath[block].reshape(rows, cl), work[g], (((0,), (0,)), ((), ())), preferred_element_type=jnp.float32
        )

    def product_of(block):
        total = times_work(block, 0)
        for k, s in shares_of(block):
            h = lax.div(s, 2)
            part = total[k * share:(k + 1) * share]

            @pl.when(lax.rem(s, 2) != core)
            def _():
                to_mate[h] = part
                mate_copy(h).start()

            @pl.when(lax.rem(s, 2) == core)
            def _():
                mine[h] = part

        for k, s in shares_of(block):
            h = lax.div(s, 2)

            @pl.when(lax.rem(s, 2) == core)
            def _():
                landed(from_mate.at[h], mate_recv.at[h])

                @pl.when(h != chip)
                def _():
                    to_chip[h] = (mine[h] + from_mate[h]).astype(to_chip.dtype)
                    chip_copy(h).start()

    def product_for_end():
        total = times_work(far, 1)
        for k, s in shares_of(far):
            part = total[k * share:(k + 1) * share]

            @pl.when(lax.rem(s, 2) != core)
            def _():
                to_mate_far[...] = part
                mate_copy_far().start()

            @pl.when(lax.rem(s, 2) == core)
            def _():
                mine_far[...] = part

        for k, s in shares_of(far):
            @pl.when(lax.rem(s, 2) == core)
            def _():
                landed(from_mate_far, far_recv)
                to_end[...] = (mine_far[...] + from_mate_far[...]).astype(to_end.dtype)
                end_copy(s).start()

    end_own = pltpu.make_async_copy(gath.at[end], ext[1].at[pl.ds(nbr, nbr)], own_sem.at[2])
    for d in range(1, n_mode - 1):
        if d > 1:
            pass_on(d, 0)
            pass_on(d, 1)

        if d == 1:
            @pl.when(is_helper & has_after)
            def _():
                halo(0, 1).start()

            @pl.when(is_helper & has_before)
            def _():
                halo(1, 1).start()

            @pl.when(is_helper)
            def _():
                end_own.start()

            product_of(mode)

        if d == n_mode - 2:
            @pl.when(is_helper)
            def _():
                product_for_end()

        @pl.when(mode >= d)
        def _():
            product_of(mode - d)

        @pl.when(mode + d < n_mode)
        def _():
            product_of(mode + d)

        if d == 1:
            @pl.when(is_helper)
            def _():
                end_own.wait()
                halo_landed(1)
                lax.fori_loop(0, nbr, functools.partial(block_row, 1), 0)

    def reduced_here(s):
        return jnp.logical_not(is_end & (lax.div(s, per_block) == far))

    def put(total):
        for q in range(2):
            out[q] = total[:, q * cl:(q + 1) * cl]

    @pl.when(reduced_here(edge))
    def _():
        total = mine[chip] + from_mate[chip]
        for step in range(1, n_chip):
            other = lax.rem(chip + step, n_chip)
            landed(from_chip.at[other], chip_recv.at[other])
            total = total + from_chip[other].astype(jnp.float32)
        put(total)

    @pl.when(jnp.logical_not(reduced_here(edge)))
    def _():
        for other in range(n_chip):
            landed(from_helper.at[other], end_recv.at[other])
        total = from_helper[0].astype(jnp.float32)
        for other in range(1, n_chip):
            total = total + from_helper[other].astype(jnp.float32)
        put(total)

    for side, there in ((0, has_after), (1, has_before)):
        @pl.when(there)
        def _():
            halo(side).wait_send()

        @pl.when(there & is_helper)
        def _():
            halo(side, 1).wait_send()

    for d in range(n_mode - 2):
        @pl.when(has_right & (mode >= d))
        def _():
            for c in range(2):
                go_right(d, c).wait_send()

        @pl.when(has_left & (mode + d < n_mode))
        def _():
            for c in range(2):
                go_left(d, c).wait_send()

    for h in range(n_chip):
        @pl.when(reduced_here(2 * h + 1 - core))
        def _():
            mate_copy(h).wait_send()

        @pl.when((h != chip) & reduced_here(2 * h + core))
        def _():
            chip_copy(h).wait_send()

    for k, s in shares_of(far):
        @pl.when(is_helper & (lax.rem(s, 2) != core))
        def _():
            mate_copy_far().wait_send()

        @pl.when(is_helper & (lax.rem(s, 2) == core))
        def _():
            end_copy(s).wait_send()


def per_device(n_edge, n_mode, basis, motional, block_cols, block_counts):
    rows, cl = basis.shape
    nbr, nnz = block_cols.shape
    bs = motional.shape[-1]
    share = cl * n_mode // n_edge
    n_chip = n_edge // 2
    part = (n_chip, share, 2 * cl)
    dma = pltpu.SemaphoreType.DMA
    return pl.pallas_call(
        functools.partial(kernel, n_edge, n_mode),
        out_shape=jax.ShapeDtypeStruct((2, share, cl), jnp.float32),
        in_specs=[
            pl.BlockSpec(memory_space=pltpu.SMEM),
            pl.BlockSpec(memory_space=pltpu.SMEM),
            pl.BlockSpec(memory_space=pl.ANY),
            pl.BlockSpec(memory_space=pl.ANY),
        ],
        out_specs=pl.BlockSpec(memory_space=pltpu.VMEM),
        scratch_shapes=[
            pltpu.VMEM((3 * nbr + 1, bs, cl), jnp.bfloat16),
            pltpu.VMEM((3 * nbr + 1, bs, cl), jnp.bfloat16),
            pltpu.VMEM((n_mode, nbr, bs, cl), jnp.bfloat16),
            pltpu.VMEM((2, nbr, nnz, bs, bs), jnp.bfloat16),
            pltpu.VMEM((2, rows, 2 * cl), jnp.bfloat16),
            pltpu.VMEM(part, jnp.float32),
            pltpu.VMEM(part, jnp.float32),
            pltpu.VMEM(part, jnp.float32),
            pltpu.VMEM(part, jnp.bfloat16),
            pltpu.VMEM(part, jnp.bfloat16),
            pltpu.VMEM(part[1:], jnp.float32),
            pltpu.VMEM(part[1:], jnp.float32),
            pltpu.VMEM(part[1:], jnp.float32),
            pltpu.VMEM(part[1:], jnp.bfloat16),
            pltpu.VMEM(part, jnp.bfloat16),
            dma((3,)),
            dma((nbr,)),
            dma((2, 2)),
            dma((2, 2)),
            dma((n_mode, 2)),
            dma((n_mode, 2)),
            dma((n_mode, 2)),
            dma((n_mode, 2)),
            dma((n_chip,)),
            dma((n_chip,)),
            dma((n_chip,)),
            dma((n_chip,)),
            dma((2,)),
            dma(()),
            dma((n_chip,)),
        ],
        compiler_params=pltpu.CompilerParams(
            collective_id=0, has_side_effects=True, vmem_limit_bytes=60 * 2**20
        ),
    )(block_cols, block_counts, basis.reshape(nbr, bs, cl), motional)


def solution(mesh):
    placed = (
        P(("geom", "edge"), "mode"),
        P("geom", "edge", None, None, None),
        P(("geom", "edge"), None),
        P(("geom", "edge")),
    )
    return jax.shard_map(
        functools.partial(per_device, mesh.shape["edge"], mesh.shape["mode"]),
        mesh=mesh, in_specs=placed, out_specs=P("geom", "edge", "mode"), check_vma=False,
    )
```

```python
import functools

import jax
import jax.numpy as jnp
from jax import lax
from jax.experimental import pallas as pl
from jax.experimental.pallas import tpu as pltpu
from jax.sharding import PartitionSpec as P

MESH = pl.DeviceIdType.MESH


def kernel(
    n_edge, n_mode,
    cols_ref, counts_ref, basis, motional, out,
    ext_own, ext_end, gath, mot, work, mine, to_mate, from_mate, to_chip, from_chip,
    mine_far, to_mate_far, from_mate_far, to_end, from_helper,
    own_sem, mot_sem, halo_send, halo_recv, right_send, right_recv, left_send, left_recv,
    mate_send, mate_recv, chip_send, chip_recv, far_send, far_recv, end_recv,
):
    ext = (ext_own, ext_end)
    edge, mode = lax.axis_index("edge"), lax.axis_index("mode")
    nbr, bs, cl = basis.shape
    nnz = mot.shape[2]
    rows = nbr * bs
    n_chip = n_edge // 2
    share = mine.shape[1]
    per_block = cl // share
    chip, core = lax.div(edge, 2), lax.rem(edge, 2)
    mate = edge + 1 - 2 * core
    is_end = (mode == 0) | (mode == n_mode - 1)
    is_helper = (mode == 1) | (mode == n_mode - 2)
    low = (mode < 2).astype(jnp.int32)
    end = (n_mode - 1) * (1 - low)
    far = (n_mode - 1) * low
    helper = end + 2 * low - 1

    barrier = pltpu.get_barrier_semaphore()
    for step in range(1, n_edge):
        pl.semaphore_signal(barrier, inc=1, device_id={"edge": lax.rem(edge + step, n_edge)}, device_id_type=MESH)
    has_left, has_right = mode > 0, mode < n_mode - 1
    has_before, has_after = edge > 0, edge < n_edge - 1

    @pl.when(has_left)
    def _():
        pl.semaphore_signal(barrier, inc=1, device_id={"mode": mode - 1}, device_id_type=MESH)

    @pl.when(has_right)
    def _():
        pl.semaphore_signal(barrier, inc=1, device_id={"mode": mode + 1}, device_id_type=MESH)

    for step in range(1, n_edge):
        to = lax.rem(edge + step, n_edge)

        @pl.when(is_end)
        def _():
            pl.semaphore_signal(barrier, inc=1, device_id={"edge": to, "mode": helper}, device_id_type=MESH)

        @pl.when(is_helper)
        def _():
            pl.semaphore_signal(barrier, inc=1, device_id={"edge": to, "mode": end}, device_id_type=MESH)

    own = [
        pltpu.make_async_copy(basis, ext[0].at[pl.ds(nbr, nbr)], own_sem.at[0]),
        pltpu.make_async_copy(basis, gath.at[mode], own_sem.at[1]),
    ]

    def mot_copy(r):
        return pltpu.make_async_copy(motional.at[:, r], mot.at[:, r], mot_sem.at[r])

    for copy in own:
        copy.start()
    for r in range(nbr):
        mot_copy(r).start()
    for g in range(2):
        ext[g][3 * nbr] = jnp.zeros((bs, cl), jnp.bfloat16)

    crossing = (n_edge - 1) * (is_end | is_helper).astype(jnp.int32)
    pl.semaphore_wait(barrier, n_edge - 1 + has_left.astype(jnp.int32) + has_right.astype(jnp.int32) + crossing)

    def half(c):
        return pl.ds(c * (nbr // 2), nbr // 2)

    def go_right(d, c):
        block = mode - d
        return pltpu.make_async_remote_copy(
            src_ref=basis.at[half(c)] if d == 0 else gath.at[block, half(c)], dst_ref=gath.at[block, half(c)],
            send_sem=right_send.at[d, c], recv_sem=right_recv.at[d, c],
            device_id={"mode": mode + 1}, device_id_type=MESH,
        )

    def go_left(d, c):
        block = mode + d
        return pltpu.make_async_remote_copy(
            src_ref=basis.at[half(c)] if d == 0 else gath.at[block, half(c)], dst_ref=gath.at[block, half(c)],
            send_sem=left_send.at[d, c], recv_sem=left_recv.at[d, c],
            device_id={"mode": mode - 1}, device_id_type=MESH,
        )

    def halo(side):
        return pltpu.make_async_remote_copy(
            src_ref=basis, dst_ref=ext_own.at[pl.ds(2 * nbr * side, nbr)],
            send_sem=halo_send.at[0, side], recv_sem=halo_recv.at[0, side],
            device_id={"edge": edge + 1 - 2 * side}, device_id_type=MESH,
        )

    def halo_end(side, c):
        return pltpu.make_async_remote_copy(
            src_ref=gath.at[end, half(c)], dst_ref=ext_end.at[pl.ds(2 * nbr * side + c * (nbr // 2), nbr // 2)],
            send_sem=halo_send.at[1 + c, side], recv_sem=halo_recv.at[1 + c, side],
            device_id={"edge": edge + 1 - 2 * side}, device_id_type=MESH,
        )

    def landed(dst, sem):
        pltpu.make_async_copy(dst, dst, sem).wait()

    @pl.when(has_after)
    def _():
        halo(0).start()

    @pl.when(has_before)
    def _():
        halo(1).start()

    for c in range(2):
        @pl.when(has_right)
        def _():
            go_right(0, c).start()

        @pl.when(has_left)
        def _():
            go_left(0, c).start()

    def pass_on(d, c):
        @pl.when(mode >= d)
        def _():
            landed(gath.at[mode - d, half(c)], right_recv.at[d - 1, c])

            if d < n_mode - 2:
                @pl.when(has_right)
                def _():
                    go_right(d, c).start()

        @pl.when(mode + d < n_mode)
        def _():
            landed(gath.at[mode + d, half(c)], left_recv.at[d - 1, c])

            if d < n_mode - 2:
                @pl.when(has_left)
                def _():
                    go_left(d, c).start()

    for copy in own:
        copy.wait()

    def halo_landed(g):
        size = nbr // 2 if g else nbr
        for c in range(1 + g):
            @pl.when(has_before)
            def _():
                landed(ext[g].at[pl.ds(c * size, size)], halo_recv.at[g + c, 0])

            @pl.when(has_after)
            def _():
                landed(ext[g].at[pl.ds(2 * nbr + c * size, size)], halo_recv.at[g + c, 1])

    halo_landed(0)
    first = edge * nbr - nbr

    def block_row(g, r, carry):
        if g == 0:
            mot_copy(r).wait()
        count = counts_ref[r]
        tiles = [
            ext[g][jnp.where(k < count, cols_ref[r, k] - first, 3 * nbr)] for k in range(nnz)
        ]
        rhs = jnp.concatenate(tiles, axis=0)
        at = pl.ds(pl.multiple_of(r * bs, bs), bs)
        for q in range(2):
            lhs = jnp.concatenate([mot[q, r, k] for k in range(nnz)], axis=1)
            product = jnp.dot(lhs, rhs, preferred_element_type=jnp.float32)
            work[g, at, q * cl:(q + 1) * cl] = product.astype(jnp.bfloat16)
        return carry

    def widen(c):
        @pl.when(is_helper & has_after)
        def _():
            halo_end(0, c).start()

        @pl.when(is_helper & has_before)
        def _():
            halo_end(1, c).start()

    lax.fori_loop(0, nbr // 2, functools.partial(block_row, 0), 0)
    pass_on(1, 0)
    widen(0)
    lax.fori_loop(nbr // 2, nbr, functools.partial(block_row, 0), 0)
    pass_on(1, 1)
    widen(1)

    def mate_copy(h):
        return pltpu.make_async_remote_copy(
            src_ref=to_mate.at[h], dst_ref=from_mate.at[h],
            send_sem=mate_send.at[h], recv_sem=mate_recv.at[h],
            device_id={"edge": mate}, device_id_type=MESH,
        )

    def chip_copy(h):
        return pltpu.make_async_remote_copy(
            src_ref=to_chip.at[h], dst_ref=from_chip.at[chip],
            send_sem=chip_send.at[h], recv_sem=chip_recv.at[chip],
            device_id={"edge": 2 * h + core}, device_id_type=MESH,
        )

    def mate_copy_far():
        return pltpu.make_async_remote_copy(
            src_ref=to_mate_far, dst_ref=from_mate_far, send_sem=far_send.at[0], recv_sem=far_recv,
            device_id={"edge": mate}, device_id_type=MESH,
        )

    def end_copy(s):
        return pltpu.make_async_remote_copy(
            src_ref=to_end, dst_ref=from_helper.at[chip], send_sem=far_send.at[1], recv_sem=end_recv.at[chip],
            device_id={"edge": s, "mode": end}, device_id_type=MESH,
        )

    def shares_of(block):
        return [(k, block * per_block + k) for k in range(per_block)]

    def times_work(block, g):
        return lax.dot_general(
            gath[block].reshape(rows, cl), work[g], (((0,), (0,)), ((), ())), preferred_element_type=jnp.float32
        )

    def product_of(block):
        total = times_work(block, 0)
        for k, s in shares_of(block):
            h = lax.div(s, 2)
            part = total[k * share:(k + 1) * share]

            @pl.when(lax.rem(s, 2) != core)
            def _():
                to_mate[h] = part
                mate_copy(h).start()

            @pl.when(lax.rem(s, 2) == core)
            def _():
                mine[h] = part

        for k, s in shares_of(block):
            h = lax.div(s, 2)

            @pl.when(lax.rem(s, 2) == core)
            def _():
                landed(from_mate.at[h], mate_recv.at[h])

                @pl.when(h != chip)
                def _():
                    to_chip[h] = (mine[h] + from_mate[h]).astype(to_chip.dtype)
                    chip_copy(h).start()

    def product_for_end():
        total = times_work(far, 1)
        for k, s in shares_of(far):
            part = total[k * share:(k + 1) * share]

            @pl.when(lax.rem(s, 2) != core)
            def _():
                to_mate_far[...] = part
                mate_copy_far().start()

            @pl.when(lax.rem(s, 2) == core)
            def _():
                mine_far[...] = part

        for k, s in shares_of(far):
            @pl.when(lax.rem(s, 2) == core)
            def _():
                landed(from_mate_far, far_recv)
                to_end[...] = (mine_far[...] + from_mate_far[...]).astype(to_end.dtype)
                end_copy(s).start()

    end_own = pltpu.make_async_copy(gath.at[end], ext[1].at[pl.ds(nbr, nbr)], own_sem.at[2])
    for d in range(1, n_mode - 1):
        if d > 1:
            pass_on(d, 0)
            pass_on(d, 1)

        if d == 1:
            @pl.when(is_helper)
            def _():
                end_own.start()

            product_of(mode)

        if d == n_mode - 2:
            @pl.when(is_helper)
            def _():
                product_for_end()

        @pl.when(mode >= d)
        def _():
            product_of(mode - d)

        @pl.when(mode + d < n_mode)
        def _():
            product_of(mode + d)

        if d == 1:
            @pl.when(is_helper)
            def _():
                end_own.wait()
                halo_landed(1)
                lax.fori_loop(0, nbr, functools.partial(block_row, 1), 0)

    def reduced_here(s):
        return jnp.logical_not(is_end & (lax.div(s, per_block) == far))

    def put(total):
        for q in range(2):
            out[q] = total[:, q * cl:(q + 1) * cl]

    @pl.when(reduced_here(edge))
    def _():
        total = mine[chip] + from_mate[chip]
        for step in range(1, n_chip):
            other = lax.rem(chip + step, n_chip)
            landed(from_chip.at[other], chip_recv.at[other])
            total = total + from_chip[other].astype(jnp.float32)
        put(total)

    @pl.when(jnp.logical_not(reduced_here(edge)))
    def _():
        for other in range(n_chip):
            landed(from_helper.at[other], end_recv.at[other])
        total = from_helper[0].astype(jnp.float32)
        for other in range(1, n_chip):
            total = total + from_helper[other].astype(jnp.float32)
        put(total)

    for side, there in ((0, has_after), (1, has_before)):
        @pl.when(there)
        def _():
            halo(side).wait_send()

        @pl.when(there & is_helper)
        def _():
            for c in range(2):
                halo_end(side, c).wait_send()

    for d in range(n_mode - 2):
        @pl.when(has_right & (mode >= d))
        def _():
            for c in range(2):
                go_right(d, c).wait_send()

        @pl.when(has_left & (mode + d < n_mode))
        def _():
            for c in range(2):
                go_left(d, c).wait_send()

    for h in range(n_chip):
        @pl.when(reduced_here(2 * h + 1 - core))
        def _():
            mate_copy(h).wait_send()

        @pl.when((h != chip) & reduced_here(2 * h + core))
        def _():
            chip_copy(h).wait_send()

    for k, s in shares_of(far):
        @pl.when(is_helper & (lax.rem(s, 2) != core))
        def _():
            mate_copy_far().wait_send()

        @pl.when(is_helper & (lax.rem(s, 2) == core))
        def _():
            end_copy(s).wait_send()


def per_device(n_edge, n_mode, basis, motional, block_cols, block_counts):
    rows, cl = basis.shape
    nbr, nnz = block_cols.shape
    bs = motional.shape[-1]
    share = cl * n_mode // n_edge
    n_chip = n_edge // 2
    part = (n_chip, share, 2 * cl)
    dma = pltpu.SemaphoreType.DMA
    return pl.pallas_call(
        functools.partial(kernel, n_edge, n_mode),
        out_shape=jax.ShapeDtypeStruct((2, share, cl), jnp.float32),
        in_specs=[
            pl.BlockSpec(memory_space=pltpu.SMEM),
            pl.BlockSpec(memory_space=pltpu.SMEM),
            pl.BlockSpec(memory_space=pl.ANY),
            pl.BlockSpec(memory_space=pl.ANY),
        ],
        out_specs=pl.BlockSpec(memory_space=pltpu.VMEM),
        scratch_shapes=[
            pltpu.VMEM((3 * nbr + 1, bs, cl), jnp.bfloat16),
            pltpu.VMEM((3 * nbr + 1, bs, cl), jnp.bfloat16),
            pltpu.VMEM((n_mode, nbr, bs, cl), jnp.bfloat16),
            pltpu.VMEM((2, nbr, nnz, bs, bs), jnp.bfloat16),
            pltpu.VMEM((2, rows, 2 * cl), jnp.bfloat16),
            pltpu.VMEM(part, jnp.float32),
            pltpu.VMEM(part, jnp.float32),
            pltpu.VMEM(part, jnp.float32),
            pltpu.VMEM(part, jnp.bfloat16),
            pltpu.VMEM(part, jnp.bfloat16),
            pltpu.VMEM(part[1:], jnp.float32),
            pltpu.VMEM(part[1:], jnp.float32),
            pltpu.VMEM(part[1:], jnp.float32),
            pltpu.VMEM(part[1:], jnp.bfloat16),
            pltpu.VMEM(part, jnp.bfloat16),
            dma((3,)),
            dma((nbr,)),
            dma((3, 2)),
            dma((3, 2)),
            dma((n_mode, 2)),
            dma((n_mode, 2)),
            dma((n_mode, 2)),
            dma((n_mode, 2)),
            dma((n_chip,)),
            dma((n_chip,)),
            dma((n_chip,)),
            dma((n_chip,)),
            dma((2,)),
            dma(()),
            dma((n_chip,)),
        ],
        compiler_params=pltpu.CompilerParams(
            collective_id=0, has_side_effects=True, vmem_limit_bytes=60 * 2**20
        ),
    )(block_cols, block_counts, basis.reshape(nbr, bs, cl), motional)


def solution(mesh):
    placed = (
        P(("geom", "edge"), "mode"),
        P("geom", "edge", None, None, None),
        P(("geom", "edge"), None),
        P(("geom", "edge")),
    )
    return jax.shard_map(
        functools.partial(per_device, mesh.shape["edge"], mesh.shape["mode"]),
        mesh=mesh, in_specs=placed, out_specs=P("geom", "edge", "mode"), check_vma=False,
    )
```
